256 devices in a mesh: dp: 16 (over z_lo, y), tensor: 16 (over x, z_hi, core).
Axes of the slice: x: 4, y: 4, z: 8 (z_hi: 2, z_lo: 4; z = z_hi * 4 + z_lo), core: 2. Of those that a mesh axis runs over, the one named last changes fastest.
Arguments:
- gradient: bfloat16 [16, 2048, 8192], P('dp', 'tensor'), may hold values from -80 to 80
- error_feed: float32 [16, 2048, 8192], P('dp', 'tensor'), may hold values from -4 to 4
- factor_old: float32 [8192, 64], P('tensor'), may hold values from -0.0625 to 0.0625
Outputs:
- error_new: float32 [16, 2048, 8192], P('dp', 'tensor')
- left_factor: float32 [2048, 64], P('tensor')
- right_factor: float32 [8192, 64], P('tensor')
The draws below stay inside these ranges and needn't reach their ends.
All inputs are finite; a program needn't handle non-finite values.
Results may differ from the reference program's by a relative error of at most 0.0003.
Values sent between devices are 32-bit elements; how exact they have to be, the bound alone decides.
No kernel may reach another device: no remote copies, remote signals or barrier semaphores. Data moves between devices by JAX's collectives and lax.ppermute only.
A program may use at most 64 MiB of HBM per device.

```python
import jax
import jax.numpy as jnp
from jax import lax

COLS = 8192
RANK = 64
ROWS = 2048
REPLICAS = 16


def draw_gradient(key, part):
    key = jax.random.fold_in(key, 11)
    keys = jax.random.split(key, 4)
    row_scale = jnp.exp(jax.random.uniform(keys[0], (1, ROWS, 1), jnp.float32, -1.15, 1.15))
    col_scale = jnp.exp(jax.random.uniform(keys[1], (1, 1, COLS), jnp.float32, -1.15, 1.15))
    values = jnp.clip(jax.random.normal(keys[3], (REPLICAS, ROWS, COLS), jnp.float32), -6.0, 6.0)
    return (values * row_scale * col_scale).astype(jnp.bfloat16)


def levels(stream_key, dims, pieces, low, top_value):
    def one(axis_at, blocks):
        draws = jax.random.uniform(jax.random.fold_in(jax.random.fold_in(stream_key, 6), axis_at), (blocks,), jnp.float32, low / len(pieces), top_value / len(pieces))
        return jnp.repeat(jnp.exp(draws), dims[axis_at] // blocks).reshape((-1,) + (1,) * (len(dims) - axis_at - 1))

    factor_of = one(*pieces[0])
    for cut in pieces[1:]:
        factor_of = factor_of * one(*cut)
    return factor_of


def bell_draw(own_key, dims, scale, most, cuts=(), held_as=jnp.bfloat16):
    drawn = scale * jax.random.normal(own_key, dims, jnp.float32)
    if cuts:
        drawn = drawn * levels(own_key, dims, cuts, -0.22, 0.18)
    return jnp.clip(drawn, -most, most).astype(held_as)


def setup_inputs(seed: int = 0) -> dict:
    seeds = jax.random.split(jax.random.key(seed), 4)
    gradient = draw_gradient(jax.random.fold_in(seeds[3], 71), 0)
    error_feed = bell_draw(seeds[1], (REPLICAS, ROWS, COLS), 0.5, 4.0, ((0, 16), (1, 16)), jnp.float32)
    factor_old = bell_draw(seeds[2], (COLS, RANK), COLS ** -0.5, 0.0625, ((0, 16),), jnp.float32)
    return dict(gradient=gradient, error_feed=error_feed, factor_old=factor_old)


def reference(gradient, error_feed, factor_old):
    highest = lax.Precision.HIGHEST

    def left_step(total, pair):
        merged = pair[0].astype(jnp.float32) + pair[1]
        return (total + jnp.dot(merged.astype(jnp.float32), factor_old.astype(jnp.float32), precision=highest, preferred_element_type=jnp.float32), None)
    left_sum, _ = lax.scan(left_step, jnp.zeros((ROWS, RANK), jnp.float32), (gradient, error_feed))
    gram = jnp.dot(left_sum.T.astype(jnp.float32), left_sum.astype(jnp.float32), precision=highest, preferred_element_type=jnp.float32)
    lower = jnp.linalg.cholesky(gram)
    left_factor = jax.scipy.linalg.solve_triangular(lower, left_sum.T, lower=True).T

    def right_step(total, pair):
        merged = pair[0].astype(jnp.float32) + pair[1]
        return (total + jnp.dot(merged.T.astype(jnp.float32), left_factor.astype(jnp.float32), precision=highest, preferred_element_type=jnp.float32), None)
    right_sum, _ = lax.scan(right_step, jnp.zeros((COLS, RANK), jnp.float32), (gradient, error_feed))
    right_factor = right_sum / REPLICAS
    approx = jnp.dot(left_factor.astype(jnp.float32), right_factor.T.astype(jnp.float32), precision=highest, preferred_element_type=jnp.float32)

    def new_error(pair):
        return pair[0].astype(jnp.float32) + pair[1] - approx
    error_new = lax.map(new_error, (gradient, error_feed))
    return (error_new, left_factor, right_factor)
```

```python
import functools

import jax
import jax.numpy as jnp
import numpy as np
from jax import lax
from jax.experimental import pallas as pl
from jax.experimental.pallas import tpu as pltpu
from jax.sharding import Mesh, PartitionSpec as P

AXES = ("zlo", "y", "x", "zhi", "core")
SIZES = (4, 4, 4, 2, 2)
ROWS, COLS, RANK, BLOCK = 128, 8192, 64, 512
CHUNKS, WIDE, EXTRA = 16, 256, 16
HALF = COLS // 2
LIMIT = 48 * 1024 * 1024
F32, BF16 = jnp.float32, jnp.bfloat16
VMEM = pl.BlockSpec(memory_space=pltpu.VMEM)


def shift(value, zlo=0, y=0, x=0, zhi=0, core=0):
    pairs = []
    for source in np.ndindex(*SIZES):
        target = tuple(a ^ b for a, b in zip(source, (zlo, y, x, zhi, core)))
        pairs.append((int(np.ravel_multi_index(source, SIZES)), int(np.ravel_multi_index(target, SIZES))))
    return lax.ppermute(value, AXES, pairs)


def ring(value, axis):
    return [shift(value, **{axis: step}) for step in (1, 2, 3)]


def total(value, axis):
    one, two, three = ring(value, axis)
    return (value + one) + (two + three)


def split(value):
    high = value.astype(BF16)
    return high, (value - high.astype(F32)).astype(BF16)


def dot(left, right, contract=((1,), (0,)), precision=None):
    return lax.dot_general(left, right, (contract, ((), ())), precision=precision, preferred_element_type=F32)


def call(kernel, out_shape, **kw):
    return pl.pallas_call(
        kernel,
        out_shape=out_shape,
        compiler_params=pltpu.CompilerParams(vmem_limit_bytes=LIMIT),
        **kw,
    )


def left_kernel(slots, first, *refs):
    merged, out = refs[0], refs[-1]
    factors = refs[1:-1] if first else refs[2:-1]
    x, zhi, core = lax.axis_index("x"), lax.axis_index("zhi"), lax.axis_index("core")
    acc = jnp.zeros((2 * ROWS, 2 * RANK), F32)
    for (sx, sc), factor in zip(slots, factors):
        for sh in range(2):
            block = (x ^ sx) * 4 + (zhi ^ sh) * 2 + (core ^ sc)
            part = merged[:, pl.ds(pl.multiple_of(block * BLOCK, BLOCK), BLOCK)]
            rows = jnp.concatenate(split(part), 0)
            cols = jnp.concatenate(split(factor[sh]), 0)
            acc = acc + dot(rows, cols, ((1,), (1,)))
    both = acc[:ROWS] + acc[ROWS:]
    turned = both.T
    result = turned[:RANK] + turned[RANK:]
    out[...] = result if first else refs[1][...] + result


def left_part(slots, merged, factors, before=None):
    first = before is None
    args = [merged] + ([] if first else [before]) + list(factors)
    return call(
        functools.partial(left_kernel, slots, first),
        jax.ShapeDtypeStruct((RANK, ROWS), F32),
        in_specs=[VMEM] * len(args),
        out_specs=VMEM,
    )(*args)


def cross_kernel(flip, with_gram, merged, left, out):
    core = lax.axis_index("core") ^ flip
    high, low = split(left[...])
    lhs = jnp.concatenate([jnp.concatenate([high, high], 1), jnp.concatenate([low, low], 1)], 0)
    for chunk in range(CHUNKS):
        start = pl.multiple_of(core * HALF + chunk * WIDE, WIDE)
        rhs = jnp.concatenate(split(merged[:, pl.ds(start, WIDE)]), 0)
        both = dot(lhs, rhs)
        out[chunk * RANK : (chunk + 1) * RANK, :] = both[:RANK] + both[RANK:]
    if with_gram:
        gram = dot(left[...], left[...], ((1,), (1,)), lax.Precision.HIGHEST)
        out[CHUNKS * RANK :, :] = jnp.concatenate([gram[q * EXTRA : (q + 1) * EXTRA] for q in range(4)], 1)


def cross_part(flip, with_gram, merged, left):
    height = CHUNKS * RANK + (EXTRA if with_gram else 0)
    return call(
        functools.partial(cross_kernel, flip, with_gram),
        jax.ShapeDtypeStruct((height, WIDE), F32),
        in_specs=[VMEM] * 2,
        out_specs=VMEM,
    )(merged, left)


def pack_kernel(own, sent, received, out):
    gram = sent[CHUNKS * RANK :, :] + received[CHUNKS * RANK :, :]
    for chunk in range(CHUNKS):
        rows = slice(chunk * RANK, (chunk + 1) * RANK)
        out[chunk, :RANK] = own[rows, :] + received[rows, :]
        out[chunk, RANK:] = gram


def sum_kernel(parts, out):
    terms = [parts[i] for i in range(CHUNKS)]
    while len(terms) > 1:
        terms = [terms[i] + terms[i + 1] for i in range(0, len(terms), 2)]
    out[...] = terms[0]


def factor_kernel(summed, left, inverse, left_out):
    packed = summed[RANK:, :] * 0.25
    gram = jnp.concatenate([packed[:, q * RANK : (q + 1) * RANK] for q in range(4)], 0)
    row = lax.broadcasted_iota(jnp.int32, (RANK, RANK), 0)
    col = lax.broadcasted_iota(jnp.int32, (RANK, RANK), 1)
    work = jnp.concatenate([gram, jnp.where(row == col, 1.0, 0.0).astype(F32)], 1)
    group = 4
    done = []
    for base in range(0, RANK, group):
        top = (base // 8) * 8
        low = work[top - top :, :]
        cols = [jnp.broadcast_to(low[:, base + j : base + j + 1], low.shape) for j in range(group)]
        rows = [low[base - top + j : base - top + j + 1, :] for j in range(group)]
        cells = [[cols[j][base - top + i : base - top + i + 1, :] for j in range(i + 1)] for i in range(group)]
        inverses, ratios = [], {}
        reduced = {}
        for j in range(group):
            for i in range(j, group):
                value = cells[i][j]
                for m in range(j):
                    value = value - ratios[i, m] * reduced[j, m]
                reduced[i, j] = value
            inverses.append(1.0 / reduced[j, j])
            for i in range(j + 1, group):
                ratios[i, j] = reduced[i, j] * inverses[j]
        update = None
        for j in range(group):
            for m in range(j):
                rows[j] = rows[j] - ratios[j, m] * rows[m]
                cols[j] = cols[j] - ratios[j, m] * cols[m]
            term = cols[j] * (rows[j] * inverses[j])
            update = term if update is None else update + term
        for j in range(group):
            done.append(rows[j] * lax.rsqrt(reduced[j, j]))
        if base + group < RANK:
            work = low - update
            drop = ((base + group) // 8) * 8 - top
            work = work[drop:, :]
    inv = jnp.concatenate(done, 0)[:, RANK:]
    inverse[...] = inv
    left_out[...] = dot(inv, left[...], precision=lax.Precision.HIGHEST)


def spread_kernel(own, one, two, three, inverse, out):
    value = ((own[:RANK] + one[:RANK]) + (two[:RANK] + three[:RANK])) * (1.0 / 16.0)
    right = dot(inverse[...], value, precision=lax.Precision.HIGHEST)
    for chunk in range(CHUNKS):
        out[chunk] = right


STEP = 1024
PER = STEP // WIDE


def error_kernel(last, *refs):
    if last:
        merged, left, right, other, _, out, mine = refs
    else:
        merged, left, right, out = refs
    step = pl.program_id(0)
    flip = 1 if last else 0
    core = lax.axis_index("core") ^ flip
    high, low = split(left[...])
    lhs = jnp.concatenate([high, high, low], 0)
    for k in range(PER):
        chunk = step * PER + k
        top, bottom = split(right[chunk])
        approx = dot(lhs, jnp.concatenate([top, bottom, top], 0), ((0,), (0,)))
        start = pl.multiple_of(core * HALF + chunk * WIDE, WIDE)
        out[0, :, k * WIDE : (k + 1) * WIDE] = merged[:, pl.ds(start, WIDE)] - approx
    if last:
        block = lax.axis_index("x") * 4 + lax.axis_index("zhi") * 2 + lax.axis_index("core")
        first = 2 * (block % 8)
        here = block // 8 == core

        @pl.when((step == 0) & here)
        def _():
            mine[:, :WIDE] = right[first]
            mine[:, WIDE:] = right[first + 1]

        @pl.when((step == 0) & jnp.logical_not(here))
        def _():
            mine[:, :WIDE] = other[first]
            mine[:, WIDE:] = other[first + 1]


def error_part(merged, left, right, other=None, before=None):
    last = before is not None
    flip = 1 if last else 0
    out_spec = pl.BlockSpec(
        (1, ROWS, STEP), lambda i: (0, 0, (lax.axis_index("core") ^ flip) * (HALF // STEP) + i)
    )
    out_shape = [jax.ShapeDtypeStruct((1, ROWS, COLS), F32)]
    out_specs = [out_spec]
    args, in_specs, alias = [merged, left, right], [VMEM] * 3, {}
    if last:
        args += [other, before]
        in_specs += [VMEM, pl.BlockSpec(memory_space=pl.ANY)]
        out_shape.append(jax.ShapeDtypeStruct((RANK, BLOCK), F32))
        out_specs.append(VMEM)
        alias = {4: 0}
    return call(
        functools.partial(error_kernel, last),
        out_shape,
        grid=(HALF // STEP,),
        in_specs=in_specs,
        out_specs=out_specs,
        input_output_aliases=alias,
    )(*args)


def exchange(value):
    return lax.all_to_all(value, ("x", "y"), split_axis=0, concat_axis=0, tiled=True)


def body(gradient, error_feed, factor_old):
    with jax.named_scope("gather_factor"):
        own = factor_old.T
        pair = jnp.stack([own, shift(own, zlo=2, zhi=1)])
        held = [pair] + ring(pair, "x")
        other = [shift(part, core=1) for part in held]
    merged = gradient[0].astype(F32) + error_feed[0]
    with jax.named_scope("left_sum"):
        part = left_part([(0, 0), (0, 1)], merged, [held[0], other[0]])
        slots = [(s, c) for c in (0, 1) for s in (1, 2, 3)]
        part = left_part(slots, merged, held[1:] + other[1:], part)
        left_sum = total(total(part, "y"), "zlo")
    with jax.named_scope("right_sum"):
        sent = cross_part(1, True, merged, left_sum)
        received = shift(sent, core=1)
        kept = cross_part(0, False, merged, left_sum)
        packed = call(
            pack_kernel,
            jax.ShapeDtypeStruct((CHUNKS, RANK + EXTRA, WIDE), F32),
            in_specs=[VMEM] * 3,
            out_specs=VMEM,
        )(kept, sent, received)
        swapped = exchange(packed)
        summed = call(
            sum_kernel,
            jax.ShapeDtypeStruct((RANK + EXTRA, WIDE), F32),
            in_specs=[VMEM],
            out_specs=VMEM,
        )(swapped)
        summed = summed + shift(summed, zlo=2, zhi=1)
        one, two, three = ring(summed, "zlo")
    with jax.named_scope("cholesky"):
        inverse, left_turned = call(
            factor_kernel,
            [jax.ShapeDtypeStruct((RANK, RANK), F32), jax.ShapeDtypeStruct((RANK, ROWS), F32)],
            in_specs=[VMEM] * 2,
            out_specs=[VMEM] * 2,
        )(summed, left_sum)
    with jax.named_scope("right_factor"):
        spread = call(
            spread_kernel,
            jax.ShapeDtypeStruct((CHUNKS, RANK, WIDE), F32),
            in_specs=[VMEM] * 5,
            out_specs=VMEM,
        )(summed, one, two, three, inverse)
        right = exchange(spread)
        right_other = shift(right, core=1)
    with jax.named_scope("error"):
        (part,) = error_part(merged, left_turned, right)
        error_new, right_turned = error_part(merged, left_turned, right_other, right, part)
    return (error_new, left_turned.T, right_turned.T)


def solution(mesh):
    fine = Mesh(mesh.devices.reshape(SIZES), AXES)
    rows = ("x", "zhi", "core")
    return jax.shard_map(
        body,
        mesh=fine,
        in_specs=(P(("zlo", "y"), rows, None), P(("zlo", "y"), rows, None), P(rows, None)),
        out_specs=(P(("zlo", "y"), rows, None), P(rows, None), P(rows, None)),
        check_vma=False,
    )
```

```python
import functools

import jax
import jax.numpy as jnp
import numpy as np
from jax import lax
from jax.experimental import pallas as pl
from jax.experimental.pallas import tpu as pltpu
from jax.sharding import Mesh, PartitionSpec as P

AXES = ("zlo", "y", "x", "zhi", "core")
SIZES = (4, 4, 4, 2, 2)
ROWS, COLS, RANK, BLOCK = 128, 8192, 64, 512
HALF = COLS // 2
WIDE, LANES, EXTRA, RING = 256, 128, 16, 4
STEPS = (1, 3, 2)
PACKED = (2, 3, 1)
TALL, GRAM = RING * RANK, 2 * EXTRA
CHUNKS = HALF // WIDE
LIMIT = 8 * 1024 * 1024
F32, BF16 = jnp.float32, jnp.bfloat16
VMEM = pl.BlockSpec(memory_space=pltpu.VMEM)


def shift(value, zlo=0, y=0, x=0, zhi=0, core=0):
    pairs = []
    for source in np.ndindex(*SIZES):
        target = tuple(a ^ b for a, b in zip(source, (zlo, y, x, zhi, core)))
        pairs.append((int(np.ravel_multi_index(source, SIZES)), int(np.ravel_multi_index(target, SIZES))))
    return lax.ppermute(value, AXES, pairs)


def ring(value, axis):
    return [shift(value, **{axis: step}) for step in STEPS]


def total(value, axis):
    one, three, two = ring(value, axis)
    return (value + one) + (three + two)


def split(value):
    high = value.astype(BF16)
    return high, (value - high.astype(F32)).astype(BF16)


def dot(left, right, contract=((1,), (0,)), precision=None):
    return lax.dot_general(left, right, (contract, ((), ())), precision=precision, preferred_element_type=F32)


def call(kernel, out_shape, **kw):
    return pl.pallas_call(
        kernel,
        out_shape=out_shape,
        compiler_params=pltpu.CompilerParams(vmem_limit_bytes=LIMIT),
        **kw,
    )


def left_kernel(slots, first, *refs):
    merged, out = refs[-2:]
    factors = refs[:-2] if first else refs[1:-2]
    x, zhi, core = lax.axis_index("x"), lax.axis_index("zhi"), lax.axis_index("core")
    acc = jnp.zeros((2 * ROWS, 2 * RANK), F32)
    for (sx, sh, sc), factor in zip(slots, factors):
        block = (x ^ sx) * 4 + (zhi ^ sh) * 2 + (core ^ sc)
        part = merged[:, pl.ds(pl.multiple_of(block * BLOCK, BLOCK), BLOCK)]
        rows = jnp.concatenate(split(part), 0)
        cols = jnp.concatenate(split(factor[...]), 0)
        acc = acc + dot(rows, cols, ((1,), (1,)))
    both = acc[:ROWS] + acc[ROWS:]
    turned = both.T
    result = turned[:RANK] + turned[RANK:]
    out[...] = result if first else refs[0][...] + result


def left_part(slots, merged, factors, before=None):
    first = before is None
    args = ([] if first else [before]) + list(factors) + [merged]
    return call(
        functools.partial(left_kernel, slots, first),
        jax.ShapeDtypeStruct((RANK, ROWS), F32),
        in_specs=[VMEM] * len(args),
        out_specs=VMEM,
    )(*args)


def column(half, chunk):
    return pl.multiple_of(half * HALF + chunk * WIDE, WIDE)


def cross_kernel(flip, merged, left, by_x, by_y):
    half = lax.axis_index("core") ^ flip
    x, y = lax.axis_index("x"), lax.axis_index("y")
    high, low = split(left[...])
    lhs = jnp.concatenate([jnp.concatenate([high, high], 1), jnp.concatenate([low, low], 1)], 0)
    gram = dot(left[...], left[...], ((1,), (1,)), lax.Precision.HIGHEST)
    flat = jnp.concatenate([gram[:GRAM], gram[GRAM:]], 1)
    for sx in range(RING):
        for sy in range(RING):
            start = column(half, (x ^ sx) * RING + (y ^ sy))
            rhs = jnp.concatenate(split(merged[:, pl.ds(start, WIDE)]), 0)
            both = dot(lhs, rhs)
            both = both[:RANK] + both[RANK:]
            by_x[sx, sy * RANK : (sy + 1) * RANK] = both[:, :LANES]
            by_y[sy, sx * RANK : (sx + 1) * RANK] = both[:, LANES:]
        by_x[sx, TALL:] = flat


def cross_part(flip, merged, left):
    return call(
        functools.partial(cross_kernel, flip),
        [
            jax.ShapeDtypeStruct((RING, TALL + GRAM, LANES), F32),
            jax.ShapeDtypeStruct((RING, TALL, LANES), F32),
        ],
        in_specs=[VMEM] * 2,
        out_specs=[VMEM] * 2,
    )(merged, left)


def pack_kernel(own, received, *outs):
    for step, out in zip((0,) + PACKED, outs):
        out[...] = own[step] + received[step]


def scatter_kernel(own, two, three, one, *outs):
    def summed(rows):
        return (own[rows] + one[rows]) + (three[rows] + two[rows])

    for step, out in zip((0,) + PACKED, outs):
        out[...] = summed(slice(step * RANK, (step + 1) * RANK))
    if len(outs) > RING:
        outs[RING][...] = summed(slice(TALL, TALL + GRAM))


def join_kernel(own_a, two_a, three_a, one_a, own_b, two_b, three_b, one_b, gram, out):
    out[:RANK, :LANES] = (own_a[...] + one_a[...]) + (three_a[...] + two_a[...])
    out[:RANK, LANES:] = (own_b[...] + one_b[...]) + (three_b[...] + two_b[...])
    out[RANK:, :LANES] = gram[:EXTRA]
    out[RANK:, LANES:] = gram[EXTRA:]


def pair_kernel(own, other, out, gram):
    out[...] = own[:RANK] + other[:RANK]
    gram[...] = own[RANK:] + other[RANK:]


def factor_kernel(packed, left, inverse, left_out, wide_out):
    flat = jnp.concatenate([packed[:, :LANES], packed[:, LANES:]], 0)
    gram = jnp.concatenate([flat[:, :RANK], flat[:, RANK:]], 0)
    row = lax.broadcasted_iota(jnp.int32, (RANK, RANK), 0)
    col = lax.broadcasted_iota(jnp.int32, (RANK, RANK), 1)
    work = jnp.concatenate([gram, jnp.where(row == col, 1.0, 0.0).astype(F32)], 1)
    group = 4
    done = []
    for base in range(0, RANK, group):
        top = (base // 8) * 8
        low = work[top - top :, :]
        cols = [jnp.broadcast_to(low[:, base + j : base + j + 1], low.shape) for j in range(group)]
        rows = [low[base - top + j : base - top + j + 1, :] for j in range(group)]
        cells = [[cols[j][base - top + i : base - top + i + 1, :] for j in range(i + 1)] for i in range(group)]
        inverses, ratios = [], {}
        reduced = {}
        for j in range(group):
            for i in range(j, group):
                value = cells[i][j]
                for m in range(j):
                    value = value - ratios[i, m] * reduced[j, m]
                reduced[i, j] = value
            inverses.append(1.0 / reduced[j, j])
            for i in range(j + 1, group):
                ratios[i, j] = reduced[i, j] * inverses[j]
        update = None
        for j in range(group):
            for m in range(j):
                rows[j] = rows[j] - ratios[j, m] * rows[m]
                cols[j] = cols[j] - ratios[j, m] * cols[m]
            term = cols[j] * (rows[j] * inverses[j])
            update = term if update is None else update + term
        for j in range(group):
            done.append(rows[j] * lax.rsqrt(reduced[j, j]))
        if base + group < RANK:
            work = low - update
            drop = ((base + group) // 8) * 8 - top
            work = work[drop:, :]
    inv = jnp.concatenate(done, 0)[:, RANK:]
    inverse[...] = inv
    turned = dot(inv, left[...], precision=lax.Precision.HIGHEST)
    left_out[...] = turned
    high, low = split(turned.T)
    wide_out[...] = jnp.concatenate([high, high, low], 1)


def spread_kernel(own, one, three, two, inverse, out):
    value = ((own[...] + one[...]) + (three[...] + two[...])) * (1.0 / 16.0)
    right = dot(inverse[...], value, precision=lax.Precision.HIGHEST)
    for chunk in range(CHUNKS):
        out[chunk] = right


def error_kernel(last, *refs):
    refs = list(refs)
    before = refs.pop(0) if last else None
    merged, left, right = refs[:3]
    out, buffer, sems = refs[3 + last], refs[-2], refs[-1]
    half = lax.axis_index("core") ^ last
    copies = []
    if last:
        other, mine = refs[3], refs[5]
        block = lax.axis_index("x") * 4 + lax.axis_index("zhi") * 2 + lax.axis_index("core")
        here = block // 8 == half
        own_copies = [[], []]
        for source, into in zip((right, other), own_copies):
            for k in range(2):
                into.append(
                    pltpu.make_async_copy(
                        source.at[2 * (block % 8) + k],
                        mine.at[:, pl.ds(k * WIDE, WIDE)],
                        sems.at[CHUNKS + k],
                    )
                )

        @pl.when(here)
        def _():
            for copy in own_copies[0]:
                copy.start()

        @pl.when(jnp.logical_not(here))
        def _():
            for copy in own_copies[1]:
                copy.start()

    for chunk in range(CHUNKS):
        top, bottom = split(right[chunk])
        approx = dot(left[...], jnp.concatenate([top, bottom, top], 0))
        start = column(half, chunk)
        buffer[chunk] = merged[:, pl.ds(start, WIDE)] - approx
        copy = pltpu.make_async_copy(buffer.at[chunk], out.at[0, :, pl.ds(start, WIDE)], sems.at[chunk])
        copy.start()
        copies.append(copy)
    for copy in copies:
        copy.wait()
    if last:

        @pl.when(here)
        def _():
            for copy in own_copies[0]:
                copy.wait()

        @pl.when(jnp.logical_not(here))
        def _():
            for copy in own_copies[1]:
                copy.wait()


def error_part(merged, left, right, other=None, before=None):
    last = before is not None
    anywhere = pl.BlockSpec(memory_space=pl.ANY)
    args = ([before] if last else []) + [merged, left, right] + ([other] if last else [])
    out_shape = [jax.ShapeDtypeStruct((1, ROWS, COLS), F32)]
    if last:
        out_shape.append(jax.ShapeDtypeStruct((RANK, BLOCK), F32))
    return call(
        functools.partial(error_kernel, int(last)),
        out_shape,
        in_specs=([anywhere] if last else []) + [VMEM] * (4 if last else 3),
        out_specs=[anywhere] * len(out_shape),
        scratch_shapes=[pltpu.VMEM((CHUNKS, ROWS, WIDE), F32), pltpu.SemaphoreType.DMA((CHUNKS + 2,))],
        input_output_aliases={0: 0} if last else {},
    )(*args)


def exchange(value):
    return lax.all_to_all(value, ("x", "y"), split_axis=0, concat_axis=0, tiled=True)


def simple(kernel, shapes, *args):
    many = isinstance(shapes, list)
    structs = [jax.ShapeDtypeStruct(shape, F32) for shape in (shapes if many else [shapes])]
    specs = [VMEM] * len(structs)
    return call(
        kernel,
        structs if many else structs[0],
        in_specs=[VMEM] * len(args),
        out_specs=specs if many else VMEM,
    )(*args)


def body(gradient, error_feed, factor_old):
    merged = gradient[0].astype(F32) + error_feed[0]
    with jax.named_scope("gather_factor"):
        own = factor_old.T
        near = ring(own, "x")
        far = shift(own, zlo=2, zhi=1)
        far, _ = lax.optimization_barrier((far, merged))
        second = ring(far, "x")
        near[0], near[1], near[2], second[2] = lax.optimization_barrier((*near, second[2]))
    with jax.named_scope("left_sum"):
        held = near + [own] + [shift(value, core=1) for value in [own] + near] + [far, shift(far, core=1)]
        slots = [(s, 0, 0) for s in STEPS] + [(0, 0, 0), (0, 0, 1)] + [(s, 0, 1) for s in STEPS]
        part = left_part(slots + [(0, 1, 0), (0, 1, 1)], merged, held)
        held = second + [shift(value, core=1) for value in second]
        part = left_part([(s, 1, c) for c in (0, 1) for s in STEPS], merged, held, part)
        left_sum = total(total(part, "y"), "zlo")
    with jax.named_scope("right_sum"):
        sent = cross_part(1, merged, left_sum)
        received = [shift(value, core=1) for value in sent]
        kept = cross_part(0, merged, left_sum)
        axes, groups = ("x", "y"), []
        for axis, own, other, height in zip(axes, kept, received, (TALL + GRAM, TALL)):
            own, *outgoing = simple(pack_kernel, [(height, LANES)] * RING, own, other)
            groups.append([own] + [shift(v, **{axis: step}) for step, v in zip(PACKED, outgoing)])
        *part_a, gram = simple(scatter_kernel, [(RANK, LANES)] * RING + [(GRAM, LANES)], *groups[0])
        part_b = simple(scatter_kernel, [(RANK, LANES)] * RING, *groups[1])
        parts = []
        for axis, (own, *outgoing) in zip(("y", "x"), (part_a, part_b)):
            parts += [own] + [shift(v, **{axis: step}) for step, v in zip(PACKED, outgoing)]
        joined = simple(join_kernel, (RANK + EXTRA, WIDE), *parts, gram)
        other = shift(joined, zlo=2, zhi=1)
        summed, gram = simple(pair_kernel, [(RANK, WIDE), (EXTRA, WIDE)], joined, other)
        others = ring(summed, "zlo")
    with jax.named_scope("cholesky"):
        inverse, left_turned, left_wide = call(
            factor_kernel,
            [
                jax.ShapeDtypeStruct((RANK, RANK), F32),
                jax.ShapeDtypeStruct((RANK, ROWS), F32),
                jax.ShapeDtypeStruct((ROWS, 3 * RANK), BF16),
            ],
            in_specs=[VMEM] * 2,
            out_specs=[VMEM] * 3,
        )(gram, left_sum)
    with jax.named_scope("right_factor"):
        right = exchange(simple(spread_kernel, (CHUNKS, RANK, WIDE), summed, *others, inverse))
        right_other = shift(right, core=1)
    with jax.named_scope("error"):
        (part,) = error_part(merged, left_wide, right)
        error_new, right_turned = error_part(merged, left_wide, right_other, right, part)
    return (error_new, left_turned.T, right_turned.T)


def solution(mesh):
    fine = Mesh(mesh.devices.reshape(SIZES), AXES)
    rows = ("x", "zhi", "core")
    return jax.shard_map(
        body,
        mesh=fine,
        in_specs=(P(("zlo", "y"), rows, None), P(("zlo", "y"), rows, None), P(rows, None)),
        out_specs=(P(("zlo", "y"), rows, None), P(rows, None), P(rows, None)),
        check_vma=False,
    )
```

```python
import functools

import jax
import jax.numpy as jnp
import numpy as np
from jax import lax
from jax.experimental import pallas as pl
from jax.experimental.pallas import tpu as pltpu
from jax.sharding import Mesh, PartitionSpec as P

AXES = ("zlo", "y", "x", "zhi", "core")
SIZES = (4, 4, 4, 2, 2)
ROWS, COLS, RANK, BLOCK = 128, 8192, 64, 512
HALF = COLS // 2
WIDE, EXTRA, RING = 256, 16, 4
STEPS = (1, 3, 2)
PACKED = (2, 3, 1)
TALL, FOLD = RING * RANK, RANK // EXTRA
CHUNKS = HALF // WIDE
LIMIT = 8 * 1024 * 1024
F32, BF16 = jnp.float32, jnp.bfloat16
VMEM = pl.BlockSpec(memory_space=pltpu.VMEM)


def moved(value, flips):
    pairs = []
    for source in np.ndindex(*SIZES):
        target = tuple(a ^ b for a, b in zip(source, flips(source[-1])))
        pairs.append((int(np.ravel_multi_index(source, SIZES)), int(np.ravel_multi_index(target, SIZES))))
    return lax.ppermute(value, AXES, pairs)


def shift(value, zlo=0, y=0, x=0, zhi=0, core=0):
    return moved(value, lambda _: (zlo, y, x, zhi, core))


def mixed(value, step, second):
    return moved(value, lambda core: (0, 0, step, 0, 0) if core == second else (0, step, 0, 0, 0))


def ring(value, axis):
    return [shift(value, **{axis: step}) for step in STEPS]


def total(value, axis):
    one, three, two = ring(value, axis)
    return (value + one) + (three + two)


def split(value):
    high = value.astype(BF16)
    return high, (value - high.astype(F32)).astype(BF16)


def dot(left, right, contract=((1,), (0,)), precision=None):
    return lax.dot_general(left, right, (contract, ((), ())), precision=precision, preferred_element_type=F32)


def call(kernel, out_shape, **kw):
    return pl.pallas_call(
        kernel,
        out_shape=out_shape,
        compiler_params=pltpu.CompilerParams(vmem_limit_bytes=LIMIT),
        **kw,
    )


def left_kernel(slots, first, *refs):
    merged, out = refs[-2:]
    factors = refs[:-2] if first else refs[1:-2]
    x, zhi, core = lax.axis_index("x"), lax.axis_index("zhi"), lax.axis_index("core")
    acc = jnp.zeros((2 * ROWS, 2 * RANK), F32)
    for (sx, sh, sc), factor in zip(slots, factors):
        block = (x ^ sx) * 4 + (zhi ^ sh) * 2 + (core ^ sc)
        part = merged[:, pl.ds(pl.multiple_of(block * BLOCK, BLOCK), BLOCK)]
        rows = jnp.concatenate(split(part), 0)
        cols = jnp.concatenate(split(factor[...]), 0)
        acc = acc + dot(rows, cols, ((1,), (1,)))
    both = acc[:ROWS] + acc[ROWS:]
    turned = both.T
    result = turned[:RANK] + turned[RANK:]
    out[...] = result if first else refs[0][...] + result


def left_part(slots, merged, factors, before=None):
    first = before is None
    args = ([] if first else [before]) + list(factors) + [merged]
    return call(
        functools.partial(left_kernel, slots, first),
        jax.ShapeDtypeStruct((RANK, ROWS), F32),
        in_specs=[VMEM] * len(args),
        out_specs=VMEM,
    )(*args)


def column(half, first, second):
    x, y = lax.axis_index("x"), lax.axis_index("y")
    along_x = (x ^ first) * RING + (y ^ second)
    along_y = (x ^ second) * RING + (y ^ first)
    return pl.multiple_of(half * HALF + jnp.where(half == 0, along_x, along_y) * WIDE, WIDE)


def cross_kernel(flip, merged, left, *outs):
    half = lax.axis_index("core") ^ flip
    high, low = split(left[...])
    lhs = jnp.concatenate([jnp.concatenate([high, high], 1), jnp.concatenate([low, low], 1)], 0)
    gram = dot(left[...], left[...], ((1,), (1,)), lax.Precision.HIGHEST)
    flat = jnp.concatenate([gram[q * EXTRA : (q + 1) * EXTRA] for q in range(FOLD)], 1)
    for index, first in enumerate((2, 3, 1, 0)):
        out, place = outs[index // 2], index % 2
        for second in range(RING):
            rhs = jnp.concatenate(split(merged[:, pl.ds(column(half, first, second), WIDE)]), 0)
            both = dot(lhs, rhs)
            out[place, second * RANK : (second + 1) * RANK] = both[:RANK] + both[RANK:]
        out[place, TALL:] = flat


def cross_part(flip, merged, left):
    return simple(functools.partial(cross_kernel, flip), [(2, TALL + EXTRA, WIDE)] * 2, merged, left)


def pack_kernel(own, received, *outs):
    for place, out in enumerate(outs):
        out[...] = own[place] + received[place]


def scatter_kernel(own, two, three, one, *outs):
    def summed(rows):
        return (own[rows] + one[rows]) + (three[rows] + two[rows])

    rows = slice(TALL, TALL + EXTRA)
    gram = jnp.where(lax.axis_index("core") == 0, summed(rows), own[rows])
    for step, out in zip((0,) + PACKED, outs):
        out[:RANK] = summed(slice(step * RANK, (step + 1) * RANK))
        out[RANK:] = gram


def join_kernel(own, two, three, one, out):
    summed = (own[...] + one[...]) + (three[...] + two[...])
    out[:RANK] = summed[:RANK]
    out[RANK:] = jnp.where(lax.axis_index("core") == 1, summed[RANK:], own[RANK:])


def pair_kernel(own, other, out, gram):
    out[...] = own[:RANK] + other[:RANK]
    gram[...] = own[RANK:] + other[RANK:]


def factor_kernel(packed, left, inverse, left_out, wide_out):
    gram = jnp.concatenate([packed[:, q * RANK : (q + 1) * RANK] for q in range(FOLD)], 0)
    row = lax.broadcasted_iota(jnp.int32, (RANK, RANK), 0)
    col = lax.broadcasted_iota(jnp.int32, (RANK, RANK), 1)
    work = jnp.concatenate([gram, jnp.where(row == col, 1.0, 0.0).astype(F32)], 1)
    group = 8
    done = []
    for base in range(0, RANK, group):
        top = (base // 8) * 8
        low = work[top - top :, :]
        cols = [jnp.broadcast_to(low[:, base + j : base + j + 1], low.shape) for j in range(group)]
        rows = [low[base - top + j : base - top + j + 1, :] for j in range(group)]
        cells = [[cols[j][base - top + i : base - top + i + 1, :] for j in range(i + 1)] for i in range(group)]
        inverses, ratios = [], {}
        reduced = {}
        for j in range(group):
            for i in range(j, group):
                value = cells[i][j]
                for m in range(j):
                    value = value - ratios[i, m] * reduced[j, m]
                reduced[i, j] = value
            inverses.append(1.0 / reduced[j, j])
            for i in range(j + 1, group):
                ratios[i, j] = reduced[i, j] * inverses[j]
        update = None
        for j in range(group):
            for m in range(j):
                rows[j] = rows[j] - ratios[j, m] * rows[m]
                cols[j] = cols[j] - ratios[j, m] * cols[m]
            term = cols[j] * (rows[j] * inverses[j])
            update = term if update is None else update + term
        for j in range(group):
            done.append(rows[j] * lax.rsqrt(reduced[j, j]))
        if base + group < RANK:
            work = low - update
            drop = ((base + group) // 8) * 8 - top
            work = work[drop:, :]
    inv = jnp.concatenate(done, 0)[:, RANK:]
    inverse[...] = inv
    turned = dot(inv, left[...], precision=lax.Precision.HIGHEST)
    left_out[...] = turned
    high, low = split(turned.T)
    wide_out[...] = jnp.concatenate([high, high, low], 1)


def spread_kernel(own, one, three, two, inverse, out):
    value = ((own[...] + one[...]) + (three[...] + two[...])) * (1.0 / 16.0)
    right = dot(inverse[...], value, precision=lax.Precision.HIGHEST)
    for chunk in range(CHUNKS):
        out[chunk] = right


def error_kernel(last, *refs):
    refs = list(refs)
    before = refs.pop(0) if last else None
    merged, left, right = refs[:3]
    out, buffer, sems = refs[3 + last], refs[-2], refs[-1]
    half = lax.axis_index("core") ^ last
    copies = []
    if last:
        other, mine = refs[3], refs[5]
        block = lax.axis_index("x") * 4 + lax.axis_index("zhi") * 2 + lax.axis_index("core")
        here = block // 8 == half
        own_copies = [[], []]
        for source, into in zip((right, other), own_copies):
            for k in range(2):
                into.append(
                    pltpu.make_async_copy(
                        source.at[2 * (block % 8) + k],
                        mine.at[:, pl.ds(k * WIDE, WIDE)],
                        sems.at[CHUNKS + k],
                    )
                )

        @pl.when(here)
        def _():
            for copy in own_copies[0]:
                copy.start()

        @pl.when(jnp.logical_not(here))
        def _():
            for copy in own_copies[1]:
                copy.start()

    for chunk in range(CHUNKS):
        top, bottom = split(right[chunk])
        approx = dot(left[...], jnp.concatenate([top, bottom, top], 0))
        start = pl.multiple_of(half * HALF + chunk * WIDE, WIDE)
        buffer[chunk] = merged[:, pl.ds(start, WIDE)] - approx
        copy = pltpu.make_async_copy(buffer.at[chunk], out.at[0, :, pl.ds(start, WIDE)], sems.at[chunk])
        copy.start()
        copies.append(copy)
    for copy in copies:
        copy.wait()
    if last:

        @pl.when(here)
        def _():
            for copy in own_copies[0]:
                copy.wait()

        @pl.when(jnp.logical_not(here))
        def _():
            for copy in own_copies[1]:
                copy.wait()


def error_part(merged, left, right, other=None, before=None):
    last = before is not None
    anywhere = pl.BlockSpec(memory_space=pl.ANY)
    args = ([before] if last else []) + [merged, left, right] + ([other] if last else [])
    out_shape = [jax.ShapeDtypeStruct((1, ROWS, COLS), F32)]
    if last:
        out_shape.append(jax.ShapeDtypeStruct((RANK, BLOCK), F32))
    return call(
        functools.partial(error_kernel, int(last)),
        out_shape,
        in_specs=([anywhere] if last else []) + [VMEM] * (4 if last else 3),
        out_specs=[anywhere] * len(out_shape),
        scratch_shapes=[pltpu.VMEM((CHUNKS, ROWS, WIDE), F32), pltpu.SemaphoreType.DMA((CHUNKS + 2,))],
        input_output_aliases={0: 0} if last else {},
    )(*args)


def exchange(value):
    return lax.all_to_all(value, ("x", "y"), split_axis=0, concat_axis=0, tiled=True)


def simple(kernel, shapes, *args):
    many = isinstance(shapes, list)
    structs = [jax.ShapeDtypeStruct(shape, F32) for shape in (shapes if many else [shapes])]
    specs = [VMEM] * len(structs)
    return call(
        kernel,
        structs if many else structs[0],
        in_specs=[VMEM] * len(args),
        out_specs=specs if many else VMEM,
    )(*args)


def body(gradient, error_feed, factor_old):
    merged = gradient[0].astype(F32) + error_feed[0]
    with jax.named_scope("gather_factor"):
        own = factor_old.T
        near = ring(own, "x")
        far = shift(own, zlo=2, zhi=1)
        far, _ = lax.optimization_barrier((far, merged))
        second = ring(far, "x")
    with jax.named_scope("left_sum"):
        held = near + [own, far]
        slots = [(s, 0) for s in STEPS] + [(0, 0), (0, 1)]
        part = left_part([slot + (0,) for slot in slots], merged, held)
        *held, last, part = lax.optimization_barrier((*held, second[2], part))
        other = [shift(value, core=1) for value in held]
        part = left_part([slot + (1,) for slot in slots] + [(2, 1, 0)], merged, other + [last], part)
        second = second[:2] + [last]
        other = [shift(value, core=1) for value in second]
        slots = [(s, 1) for s in STEPS]
        slots = [slot + (0,) for slot in slots[:2]] + [slot + (1,) for slot in slots]
        part = left_part(slots, merged, second[:2] + other, part)
        left_sum = total(total(part, "y"), "zlo")
    with jax.named_scope("right_sum"):
        sent = cross_part(1, merged, left_sum)
        received = [shift(value, core=1) for value in sent]
        kept = cross_part(0, merged, left_sum)
        packed = []
        for mine, theirs in zip(kept, received):
            packed += simple(pack_kernel, [(TALL + EXTRA, WIDE)] * 2, mine, theirs)
        *outgoing, own = packed
        incoming = [mixed(value, step, 0) for step, value in zip(PACKED, outgoing)]
        own, *outgoing = simple(scatter_kernel, [(RANK + EXTRA, WIDE)] * RING, own, *incoming)
        incoming = [mixed(value, step, 1) for step, value in zip(PACKED, outgoing)]
        joined = simple(join_kernel, (RANK + EXTRA, WIDE), own, *incoming)
        other = shift(joined, zlo=2, zhi=1)
        summed, gram = simple(pair_kernel, [(RANK, WIDE), (EXTRA, WIDE)], joined, other)
        others = ring(summed, "zlo")
    with jax.named_scope("cholesky"):
        inverse, left_turned, left_wide = call(
            factor_kernel,
            [
                jax.ShapeDtypeStruct((RANK, RANK), F32),
                jax.ShapeDtypeStruct((RANK, ROWS), F32),
                jax.ShapeDtypeStruct((ROWS, 3 * RANK), BF16),
            ],
            in_specs=[VMEM] * 2,
            out_specs=[VMEM] * 3,
        )(gram, left_sum)
    with jax.named_scope("right_factor"):
        right = exchange(simple(spread_kernel, (CHUNKS, RANK, WIDE), summed, *others, inverse))
        right_other = shift(right, core=1)
    with jax.named_scope("error"):
        (part,) = error_part(merged, left_wide, right)
        error_new, right_turned = error_part(merged, left_wide, right_other, right, part)
    return (error_new, left_turned.T, right_turned.T)


def solution(mesh):
    fine = Mesh(mesh.devices.reshape(SIZES), AXES)
    rows = ("x", "zhi", "core")
    return jax.shard_map(
        body,
        mesh=fine,
        in_specs=(P(("zlo", "y"), rows, None), P(("zlo", "y"), rows, None), P(rows, None)),
        out_specs=(P(("zlo", "y"), rows, None), P(rows, None), P(rows, None)),
        check_vma=False,
    )
```

```python
import functools

import jax
import jax.numpy as jnp
import numpy as np
from jax import lax
from jax.experimental import pallas as pl
from jax.experimental.pallas import tpu as pltpu
from jax.sharding import Mesh, PartitionSpec as P

AXES = ("zlo", "y", "x", "zhi", "core")
SIZES = (4, 4, 4, 2, 2)
ROWS, COLS, RANK, BLOCK = 128, 8192, 64, 512
HALF = COLS // 2
WIDE, EXTRA, RING = 256, 16, 4
STEPS = (1, 3, 2)
PACKED = (2, 3, 1)
TALL, FOLD = RING * RANK, RANK // EXTRA
CHUNKS = HALF // WIDE
LIMIT = 8 * 1024 * 1024
F32, BF16 = jnp.float32, jnp.bfloat16
VMEM = pl.BlockSpec(memory_space=pltpu.VMEM)


def moved(value, flips):
    pairs = []
    for source in np.ndindex(*SIZES):
        target = tuple(a ^ b for a, b in zip(source, flips(source[-1])))
        pairs.append((int(np.ravel_multi_index(source, SIZES)), int(np.ravel_multi_index(target, SIZES))))
    return lax.ppermute(value, AXES, pairs)


def shift(value, zlo=0, y=0, x=0, zhi=0, core=0):
    return moved(value, lambda _: (zlo, y, x, zhi, core))


def mixed(value, step, second):
    return moved(value, lambda core: (0, 0, step, 0, 0) if core == second else (0, step, 0, 0, 0))


def ring(value, axis):
    return [shift(value, **{axis: step}) for step in STEPS]


def total(value, on_y):
    one, three, two = [
        moved(value, lambda core: (0, step, 0, 0, 0) if core == on_y else (step, 0, 0, 0, 0))
        for step in STEPS
    ]
    return (value + one) + (three + two)


def split(value):
    high = value.astype(BF16)
    return high, (value - high.astype(F32)).astype(BF16)


def dot(left, right, contract=((1,), (0,)), precision=None):
    return lax.dot_general(left, right, (contract, ((), ())), precision=precision, preferred_element_type=F32)


def call(kernel, out_shape, **kw):
    return pl.pallas_call(
        kernel,
        out_shape=out_shape,
        compiler_params=pltpu.CompilerParams(vmem_limit_bytes=LIMIT),
        **kw,
    )


def left_kernel(slots, first, *refs):
    merged, out = refs[-2:]
    factors = refs[:-2] if first else refs[1:-2]
    x, zhi, core = lax.axis_index("x"), lax.axis_index("zhi"), lax.axis_index("core")
    acc = jnp.zeros((2 * ROWS, 2 * RANK), F32)
    for (sx, sh, sc), factor in zip(slots, factors):
        block = (x ^ sx) * 4 + (zhi ^ sh) * 2 + (core ^ sc)
        part = merged[:, pl.ds(pl.multiple_of(block * BLOCK, BLOCK), BLOCK)]
        rows = jnp.concatenate(split(part), 0)
        cols = jnp.concatenate(split(factor[...]), 0)
        acc = acc + dot(rows, cols, ((1,), (1,)))
    both = acc[:ROWS] + acc[ROWS:]
    turned = both.T
    result = turned[:RANK] + turned[RANK:]
    out[...] = result if first else refs[0][...] + result


def left_part(slots, merged, factors, before=None):
    first = before is None
    args = ([] if first else [before]) + list(factors) + [merged]
    return call(
        functools.partial(left_kernel, slots, first),
        jax.ShapeDtypeStruct((RANK, ROWS), F32),
        in_specs=[VMEM] * len(args),
        out_specs=VMEM,
    )(*args)


def column(half, first, second):
    x, y = lax.axis_index("x"), lax.axis_index("y")
    along_x = (x ^ first) * RING + (y ^ second)
    along_y = (x ^ second) * RING + (y ^ first)
    return pl.multiple_of(half * HALF + jnp.where(half == 0, along_x, along_y) * WIDE, WIDE)


def cross_kernel(flip, merged, left, *outs):
    half = lax.axis_index("core") ^ flip
    high, low = split(left[...])
    lhs = jnp.concatenate([jnp.concatenate([high, high], 1), jnp.concatenate([low, low], 1)], 0)
    gram = dot(left[...], left[...], ((1,), (1,)), lax.Precision.HIGHEST)
    flat = jnp.concatenate([gram[q * EXTRA : (q + 1) * EXTRA] for q in range(FOLD)], 1)
    for index, first in enumerate((2, 3, 1, 0)):
        out, place = outs[index // 2], index % 2
        for second in range(RING):
            rhs = jnp.concatenate(split(merged[:, pl.ds(column(half, first, second), WIDE)]), 0)
            both = dot(lhs, rhs)
            out[place, second * RANK : (second + 1) * RANK] = both[:RANK] + both[RANK:]
        out[place, TALL:] = flat


def cross_part(flip, merged, left):
    return simple(functools.partial(cross_kernel, flip), [(2, TALL + EXTRA, WIDE)] * 2, merged, left)


def pack_kernel(own, received, *outs):
    for place, out in enumerate(outs):
        out[...] = own[place] + received[place]


def scatter_kernel(own, two, three, one, *outs):
    def summed(rows):
        return (own[rows] + one[rows]) + (three[rows] + two[rows])

    rows = slice(TALL, TALL + EXTRA)
    gram = jnp.where(lax.axis_index("core") == 0, summed(rows), own[rows])
    for step, out in zip((0,) + PACKED, outs):
        out[:RANK] = summed(slice(step * RANK, (step + 1) * RANK))
        out[RANK:] = gram


def join_kernel(own, two, three, one, out):
    summed = (own[...] + one[...]) + (three[...] + two[...])
    out[:RANK] = summed[:RANK]
    out[RANK:] = jnp.where(lax.axis_index("core") == 1, summed[RANK:], own[RANK:])


def pair_kernel(own, other, out, gram):
    out[...] = own[:RANK] + other[:RANK]
    gram[...] = own[RANK:] + other[RANK:]


def factor_kernel(packed, left, inverse, left_out, wide_out):
    gram = jnp.concatenate([packed[:, q * RANK : (q + 1) * RANK] for q in range(FOLD)], 0)
    row = lax.broadcasted_iota(jnp.int32, (RANK, RANK), 0)
    col = lax.broadcasted_iota(jnp.int32, (RANK, RANK), 1)
    work = jnp.concatenate([gram, jnp.where(row == col, 1.0, 0.0).astype(F32)], 1)
    group = 8
    done = []
    for base in range(0, RANK, group):
        top = (base // 8) * 8
        low = work[top - top :, :]
        cols = [jnp.broadcast_to(low[:, base + j : base + j + 1], low.shape) for j in range(group)]
        rows = [low[base - top + j : base - top + j + 1, :] for j in range(group)]
        cells = [[cols[j][base - top + i : base - top + i + 1, :] for j in range(i + 1)] for i in range(group)]
        inverses, ratios = [], {}
        reduced = {}
        for j in range(group):
            for i in range(j, group):
                value = cells[i][j]
                for m in range(j):
                    value = value - ratios[i, m] * reduced[j, m]
                reduced[i, j] = value
            inverses.append(1.0 / reduced[j, j])
            for i in range(j + 1, group):
                ratios[i, j] = reduced[i, j] * inverses[j]
        update = None
        for j in range(group):
            for m in range(j):
                rows[j] = rows[j] - ratios[j, m] * rows[m]
                cols[j] = cols[j] - ratios[j, m] * cols[m]
            term = cols[j] * (rows[j] * inverses[j])
            update = term if update is None else update + term
        for j in range(group):
            done.append(rows[j] * lax.rsqrt(reduced[j, j]))
        if base + group < RANK:
            work = low - update
            drop = ((base + group) // 8) * 8 - top
            work = work[drop:, :]
    inv = jnp.concatenate(done, 0)[:, RANK:]
    inverse[...] = inv
    turned = dot(inv, left[...], precision=lax.Precision.HIGHEST)
    left_out[...] = turned
    high, low = split(turned.T)
    wide_out[...] = jnp.concatenate([high, high, low], 1)


def spread_kernel(own, one, three, two, inverse, out):
    value = ((own[...] + one[...]) + (three[...] + two[...])) * (1.0 / 16.0)
    right = dot(inverse[...], value, precision=lax.Precision.HIGHEST)
    for chunk in range(CHUNKS):
        out[chunk] = right


def error_kernel(last, *refs):
    refs = list(refs)
    before = refs.pop(0) if last else None
    merged, left, right = refs[:3]
    out, buffer, sems = refs[3 + last], refs[-2], refs[-1]
    half = lax.axis_index("core") ^ last
    copies = []
    if last:
        other, mine = refs[3], refs[5]
        block = lax.axis_index("x") * 4 + lax.axis_index("zhi") * 2 + lax.axis_index("core")
        here = block // 8 == half
        own_copies = [[], []]
        for source, into in zip((right, other), own_copies):
            for k in range(2):
                into.append(
                    pltpu.make_async_copy(
                        source.at[2 * (block % 8) + k],
                        mine.at[:, pl.ds(k * WIDE, WIDE)],
                        sems.at[CHUNKS + k],
                    )
                )

        @pl.when(here)
        def _():
            for copy in own_copies[0]:
                copy.start()

        @pl.when(jnp.logical_not(here))
        def _():
            for copy in own_copies[1]:
                copy.start()

    for chunk in range(CHUNKS):
        top, bottom = split(right[chunk])
        approx = dot(left[...], jnp.concatenate([top, bottom, top], 0))
        start = pl.multiple_of(half * HALF + chunk * WIDE, WIDE)
        buffer[chunk] = merged[:, pl.ds(start, WIDE)] - approx
        copy = pltpu.make_async_copy(buffer.at[chunk], out.at[0, :, pl.ds(start, WIDE)], sems.at[chunk])
        copy.start()
        copies.append(copy)
    for copy in copies:
        copy.wait()
    if last:

        @pl.when(here)
        def _():
            for copy in own_copies[0]:
                copy.wait()

        @pl.when(jnp.logical_not(here))
        def _():
            for copy in own_copies[1]:
                copy.wait()


def error_part(merged, left, right, other=None, before=None):
    last = before is not None
    anywhere = pl.BlockSpec(memory_space=pl.ANY)
    args = ([before] if last else []) + [merged, left, right] + ([other] if last else [])
    out_shape = [jax.ShapeDtypeStruct((1, ROWS, COLS), F32)]
    if last:
        out_shape.append(jax.ShapeDtypeStruct((RANK, BLOCK), F32))
    return call(
        functools.partial(error_kernel, int(last)),
        out_shape,
        in_specs=([anywhere] if last else []) + [VMEM] * (4 if last else 3),
        out_specs=[anywhere] * len(out_shape),
        scratch_shapes=[pltpu.VMEM((CHUNKS, ROWS, WIDE), F32), pltpu.SemaphoreType.DMA((CHUNKS + 2,))],
        input_output_aliases={0: 0} if last else {},
    )(*args)


def exchange(value):
    return lax.all_to_all(value, ("x", "y"), split_axis=0, concat_axis=0, tiled=True)


def simple(kernel, shapes, *args):
    many = isinstance(shapes, list)
    structs = [jax.ShapeDtypeStruct(shape, F32) for shape in (shapes if many else [shapes])]
    specs = [VMEM] * len(structs)
    return call(
        kernel,
        structs if many else structs[0],
        in_specs=[VMEM] * len(args),
        out_specs=specs if many else VMEM,
    )(*args)


def body(gradient, error_feed, factor_old):
    merged = gradient[0].astype(F32) + error_feed[0]
    with jax.named_scope("gather_factor"):
        own = factor_old.T
        near = ring(own, "x")
        far = shift(own, zlo=2, zhi=1)
        far, _ = lax.optimization_barrier((far, merged))
        second = ring(far, "x")
    with jax.named_scope("left_sum"):
        held = near + [own, far]
        slots = [(s, 0) for s in STEPS] + [(0, 0), (0, 1)]
        part = left_part([slot + (0,) for slot in slots], merged, held)
        *held, last, part = lax.optimization_barrier((*held, second[2], part))
        other = [shift(value, core=1) for value in held]
        part = left_part([slot + (1,) for slot in slots] + [(2, 1, 0)], merged, other + [last], part)
        second = second[:2] + [last]
        other = [shift(value, core=1) for value in second]
        slots = [(s, 1) for s in STEPS]
        slots = [slot + (0,) for slot in slots[:2]] + [slot + (1,) for slot in slots]
        part = left_part(slots, merged, second[:2] + other, part)
        left_sum = total(total(part, 1), 0)
    with jax.named_scope("right_sum"):
        sent = cross_part(1, merged, left_sum)
        received = [shift(value, core=1) for value in sent]
        kept = cross_part(0, merged, left_sum)
        packed = []
        for mine, theirs in zip(kept, received):
            packed += simple(pack_kernel, [(TALL + EXTRA, WIDE)] * 2, mine, theirs)
        *outgoing, own = packed
        incoming = [mixed(value, step, 0) for step, value in zip(PACKED, outgoing)]
        own, *outgoing = simple(scatter_kernel, [(RANK + EXTRA, WIDE)] * RING, own, *incoming)
        incoming = [mixed(value, step, 1) for step, value in zip(PACKED, outgoing)]
        joined = simple(join_kernel, (RANK + EXTRA, WIDE), own, *incoming)
        other = shift(joined, zlo=2, zhi=1)
        summed, gram = simple(pair_kernel, [(RANK, WIDE), (EXTRA, WIDE)], joined, other)
        others = ring(summed, "zlo")
    with jax.named_scope("cholesky"):
        inverse, left_turned, left_wide = call(
            factor_kernel,
            [
                jax.ShapeDtypeStruct((RANK, RANK), F32),
                jax.ShapeDtypeStruct((RANK, ROWS), F32),
                jax.ShapeDtypeStruct((ROWS, 3 * RANK), BF16),
            ],
            in_specs=[VMEM] * 2,
            out_specs=[VMEM] * 3,
        )(gram, left_sum)
    with jax.named_scope("right_factor"):
        right = exchange(simple(spread_kernel, (CHUNKS, RANK, WIDE), summed, *others, inverse))
        right_other = shift(right, core=1)
    with jax.named_scope("error"):
        (part,) = error_part(merged, left_wide, right)
        error_new, right_turned = error_part(merged, left_wide, right_other, right, part)
    return (error_new, left_turned.T, right_turned.T)


def solution(mesh):
    fine = Mesh(mesh.devices.reshape(SIZES), AXES)
    rows = ("x", "zhi", "core")
    return jax.shard_map(
        body,
        mesh=fine,
        in_specs=(P(("zlo", "y"), rows, None), P(("zlo", "y"), rows, None), P(rows, None)),
        out_specs=(P(("zlo", "y"), rows, None), P(rows, None), P(rows, None)),
        check_vma=False,
    )
```

```python
import functools

import jax
import jax.numpy as jnp
import numpy as np
from jax import lax
from jax.experimental import pallas as pl
from jax.experimental.pallas import tpu as pltpu
from jax.sharding import Mesh, PartitionSpec as P

AXES = ("zlo", "y", "x", "zhi", "core")
SIZES = (4, 4, 4, 2, 2)
ROWS, COLS, RANK, BLOCK = 128, 8192, 64, 512
HALF = COLS // 2
WIDE, EXTRA, RING = 256, 16, 4
STEPS = (1, 3, 2)
PACKED = (2, 3, 1)
TALL, FOLD = RING * RANK, RANK // EXTRA
CHUNKS = HALF // WIDE
LIMIT = 8 * 1024 * 1024
F32, BF16 = jnp.float32, jnp.bfloat16
VMEM = pl.BlockSpec(memory_space=pltpu.VMEM)


def moved(value, flips):
    pairs = []
    for source in np.ndindex(*SIZES):
        target = tuple(a ^ b for a, b in zip(source, flips(source[-1])))
        pairs.append((int(np.ravel_multi_index(source, SIZES)), int(np.ravel_multi_index(target, SIZES))))
    return lax.ppermute(value, AXES, pairs)


def shift(value, zlo=0, y=0, x=0, zhi=0, core=0):
    return moved(value, lambda _: (zlo, y, x, zhi, core))


def mixed(value, step, second):
    return moved(value, lambda core: (0, 0, step, 0, 0) if core == second else (0, step, 0, 0, 0))


def ring(value, axis):
    return [shift(value, **{axis: step}) for step in STEPS]


def total(value, on_y):
    one, three, two = [
        moved(value, lambda core: (0, step, 0, 0, 0) if core == on_y else (step, 0, 0, 0, 0))
        for step in STEPS
    ]
    return (value + one) + (three + two)


def split(value):
    high = value.astype(BF16)
    return high, (value - high.astype(F32)).astype(BF16)


def dot(left, right, contract=((1,), (0,)), precision=None):
    return lax.dot_general(left, right, (contract, ((), ())), precision=precision, preferred_element_type=F32)


def call(kernel, out_shape, **kw):
    return pl.pallas_call(
        kernel,
        out_shape=out_shape,
        compiler_params=pltpu.CompilerParams(vmem_limit_bytes=LIMIT),
        **kw,
    )


def left_kernel(slots, first, *refs):
    merged, out = refs[-2:]
    factors = refs[:-2] if first else refs[1:-2]
    x, zhi, core = lax.axis_index("x"), lax.axis_index("zhi"), lax.axis_index("core")
    acc = jnp.zeros((2 * ROWS, 2 * RANK), F32)
    for (sx, sh, sc), factor in zip(slots, factors):
        block = (x ^ sx) * 4 + (zhi ^ sh) * 2 + (core ^ sc)
        part = merged[:, pl.ds(pl.multiple_of(block * BLOCK, BLOCK), BLOCK)]
        rows = jnp.concatenate(split(part), 0)
        cols = jnp.concatenate(split(factor[...]), 0)
        acc = acc + dot(rows, cols, ((1,), (1,)))
    both = acc[:ROWS] + acc[ROWS:]
    turned = both.T
    result = turned[:RANK] + turned[RANK:]
    out[...] = result if first else refs[0][...] + result


def left_part(slots, merged, factors, before=None):
    first = before is None
    args = ([] if first else [before]) + list(factors) + [merged]
    return call(
        functools.partial(left_kernel, slots, first),
        jax.ShapeDtypeStruct((RANK, ROWS), F32),
        in_specs=[VMEM] * len(args),
        out_specs=VMEM,
    )(*args)


def column(half, first, second):
    x, y = lax.axis_index("x"), lax.axis_index("y")
    along_x = (x ^ first) * RING + (y ^ second)
    along_y = (x ^ second) * RING + (y ^ first)
    return pl.multiple_of(half * HALF + jnp.where(half == 0, along_x, along_y) * WIDE, WIDE)


def cross_kernel(flip, merged, left, *outs):
    half = lax.axis_index("core") ^ flip
    high, low = split(left[...])
    lhs = jnp.concatenate([jnp.concatenate([high, high], 1), jnp.concatenate([low, low], 1)], 0)
    gram = dot(left[...], left[...], ((1,), (1,)), lax.Precision.HIGHEST)
    flat = jnp.concatenate([gram[q * EXTRA : (q + 1) * EXTRA] for q in range(FOLD)], 1)
    for index, first in enumerate((2, 3, 1, 0)):
        out, place = outs[index // 2], index % 2
        for second in range(RING):
            rhs = jnp.concatenate(split(merged[:, pl.ds(column(half, first, second), WIDE)]), 0)
            both = dot(lhs, rhs)
            out[place, second * RANK : (second + 1) * RANK] = both[:RANK] + both[RANK:]
        if first == 0:
            out[place, TALL:] = flat


def cross_part(flip, merged, left):
    return simple(functools.partial(cross_kernel, flip), [(2, TALL, WIDE), (2, TALL + EXTRA, WIDE)], merged, left)


def pack_kernel(own, received, *outs):
    for place, out in enumerate(outs):
        rows = slice(0, out.shape[0])
        out[...] = own[place, rows] + received[place, rows]


def scatter_kernel(own, two, three, one, *outs):
    def summed(rows):
        return (own[rows] + one[rows]) + (three[rows] + two[rows])

    gram = own[TALL:]
    for step, out in zip((0,) + PACKED, outs):
        out[:RANK] = summed(slice(step * RANK, (step + 1) * RANK))
        out[RANK:] = gram


def join_kernel(own, two, three, one, out):
    summed = (own[...] + one[...]) + (three[...] + two[...])
    out[:RANK] = summed[:RANK]
    out[RANK:] = summed[RANK:]


def pair_kernel(own, other, out, gram):
    out[...] = own[:RANK] + other[:RANK]
    gram[...] = own[RANK:] + other[RANK:]


def factor_kernel(own, other, left, inverse, left_out, wide_out):
    packed = jnp.where(lax.axis_index("core") == 1, own[...], other[...])
    gram = jnp.concatenate([packed[:, q * RANK : (q + 1) * RANK] for q in range(FOLD)], 0)
    row = lax.broadcasted_iota(jnp.int32, (RANK, RANK), 0)
    col = lax.broadcasted_iota(jnp.int32, (RANK, RANK), 1)
    work = jnp.concatenate([gram, jnp.where(row == col, 1.0, 0.0).astype(F32)], 1)
    group = 8
    done = []
    for base in range(0, RANK, group):
        top = (base // 8) * 8
        low = work[top - top :, :]
        cols = [jnp.broadcast_to(low[:, base + j : base + j + 1], low.shape) for j in range(group)]
        rows = [low[base - top + j : base - top + j + 1, :] for j in range(group)]
        cells = [[cols[j][base - top + i : base - top + i + 1, :] for j in range(i + 1)] for i in range(group)]
        inverses, ratios = [], {}
        reduced = {}
        for j in range(group):
            for i in range(j, group):
                value = cells[i][j]
                for m in range(j):
                    value = value - ratios[i, m] * reduced[j, m]
                reduced[i, j] = value
            inverses.append(1.0 / reduced[j, j])
            for i in range(j + 1, group):
                ratios[i, j] = reduced[i, j] * inverses[j]
        update = None
        for j in range(group):
            for m in range(j):
                rows[j] = rows[j] - ratios[j, m] * rows[m]
                cols[j] = cols[j] - ratios[j, m] * cols[m]
            term = cols[j] * (rows[j] * inverses[j])
            update = term if update is None else update + term
        for j in range(group):
            done.append(rows[j] * lax.rsqrt(reduced[j, j]))
        if base + group < RANK:
            work = low - update
            drop = ((base + group) // 8) * 8 - top
            work = work[drop:, :]
    inv = jnp.concatenate(done, 0)[:, RANK:]
    inverse[...] = inv
    turned = dot(inv, left[...], precision=lax.Precision.HIGHEST)
    left_out[...] = turned
    high, low = split(turned.T)
    wide_out[...] = jnp.concatenate([high, high, low], 1)


def spread_kernel(own, one, three, two, inverse, out):
    value = ((own[...] + one[...]) + (three[...] + two[...])) * (1.0 / 16.0)
    right = dot(inverse[...], value, precision=lax.Precision.HIGHEST)
    for chunk in range(CHUNKS):
        out[chunk] = right


def error_kernel(last, *refs):
    refs = list(refs)
    before = refs.pop(0) if last else None
    merged, left, right = refs[:3]
    out, buffer, sems = refs[3 + last], refs[-2], refs[-1]
    half = lax.axis_index("core") ^ last
    copies = []
    if last:
        other, mine = refs[3], refs[5]
        block = lax.axis_index("x") * 4 + lax.axis_index("zhi") * 2 + lax.axis_index("core")
        here = block // 8 == half
        own_copies = [[], []]
        for source, into in zip((right, other), own_copies):
            for k in range(2):
                into.append(
                    pltpu.make_async_copy(
                        source.at[2 * (block % 8) + k],
                        mine.at[:, pl.ds(k * WIDE, WIDE)],
                        sems.at[CHUNKS + k],
                    )
                )

        @pl.when(here)
        def _():
            for copy in own_copies[0]:
                copy.start()

        @pl.when(jnp.logical_not(here))
        def _():
            for copy in own_copies[1]:
                copy.start()

    for chunk in range(CHUNKS):
        top, bottom = split(right[chunk])
        approx = dot(left[...], jnp.concatenate([top, bottom, top], 0))
        start = pl.multiple_of(half * HALF + chunk * WIDE, WIDE)
        buffer[chunk] = merged[:, pl.ds(start, WIDE)] - approx
        copy = pltpu.make_async_copy(buffer.at[chunk], out.at[0, :, pl.ds(start, WIDE)], sems.at[chunk])
        copy.start()
        copies.append(copy)
    for copy in copies:
        copy.wait()
    if last:

        @pl.when(here)
        def _():
            for copy in own_copies[0]:
                copy.wait()

        @pl.when(jnp.logical_not(here))
        def _():
            for copy in own_copies[1]:
                copy.wait()


def error_part(merged, left, right, other=None, before=None):
    last = before is not None
    anywhere = pl.BlockSpec(memory_space=pl.ANY)
    args = ([before] if last else []) + [merged, left, right] + ([other] if last else [])
    out_shape = [jax.ShapeDtypeStruct((1, ROWS, COLS), F32)]
    if last:
        out_shape.append(jax.ShapeDtypeStruct((RANK, BLOCK), F32))
    return call(
        functools.partial(error_kernel, int(last)),
        out_shape,
        in_specs=([anywhere] if last else []) + [VMEM] * (4 if last else 3),
        out_specs=[anywhere] * len(out_shape),
        scratch_shapes=[pltpu.VMEM((CHUNKS, ROWS, WIDE), F32), pltpu.SemaphoreType.DMA((CHUNKS + 2,))],
        input_output_aliases={0: 0} if last else {},
    )(*args)


def exchange(value):
    return lax.all_to_all(value, ("x", "y"), split_axis=0, concat_axis=0, tiled=True)


def simple(kernel, shapes, *args):
    many = isinstance(shapes, list)
    structs = [jax.ShapeDtypeStruct(shape, F32) for shape in (shapes if many else [shapes])]
    specs = [VMEM] * len(structs)
    return call(
        kernel,
        structs if many else structs[0],
        in_specs=[VMEM] * len(args),
        out_specs=specs if many else VMEM,
    )(*args)


def body(gradient, error_feed, factor_old):
    merged = gradient[0].astype(F32) + error_feed[0]
    with jax.named_scope("gather_factor"):
        own = factor_old.T
        near = ring(own, "x")
        far = shift(own, zlo=2, zhi=1)
        far, _ = lax.optimization_barrier((far, merged))
        second = ring(far, "x")
    with jax.named_scope("left_sum"):
        held = near + [own, far]
        slots = [(s, 0) for s in STEPS] + [(0, 0), (0, 1)]
        part = left_part([slot + (0,) for slot in slots], merged, held)
        *held, last, part = lax.optimization_barrier((*held, second[2], part))
        other = [shift(value, core=1) for value in held]
        part = left_part([slot + (1,) for slot in slots] + [(2, 1, 0)], merged, other + [last], part)
        second = second[:2] + [last]
        other = [shift(value, core=1) for value in second]
        slots = [(s, 1) for s in STEPS]
        slots = [slot + (0,) for slot in slots[:2]] + [slot + (1,) for slot in slots]
        part = left_part(slots, merged, second[:2] + other, part)
        left_sum = total(total(part, 1), 0)
    with jax.named_scope("right_sum"):
        sent = cross_part(1, merged, left_sum)
        received = [shift(value, core=1) for value in sent]
        kept = cross_part(0, merged, left_sum)
        packed = []
        for mine, theirs in zip(kept, received):
            packed += simple(pack_kernel, [(TALL, WIDE), (mine.shape[1], WIDE)], mine, theirs)
        *outgoing, own = packed
        incoming = [mixed(value, step, 0) for step, value in zip(PACKED, outgoing)]
        own, *outgoing = simple(scatter_kernel, [(RANK + EXTRA, WIDE)] * RING, own, *incoming)
        incoming = [mixed(value, step, 1) for step, value in zip(PACKED, outgoing)]
        joined = simple(join_kernel, (RANK + EXTRA, WIDE), own, *incoming)
        other = shift(joined, zlo=2, zhi=1)
        summed, gram = simple(pair_kernel, [(RANK, WIDE), (EXTRA, WIDE)], joined, other)
        others = ring(summed, "zlo")
        gram_other = shift(gram, core=1)
    with jax.named_scope("cholesky"):
        inverse, left_turned, left_wide = call(
            factor_kernel,
            [
                jax.ShapeDtypeStruct((RANK, RANK), F32),
                jax.ShapeDtypeStruct((RANK, ROWS), F32),
                jax.ShapeDtypeStruct((ROWS, 3 * RANK), BF16),
            ],
            in_specs=[VMEM] * 3,
            out_specs=[VMEM] * 3,
        )(gram, gram_other, left_sum)
    with jax.named_scope("right_factor"):
        right = exchange(simple(spread_kernel, (CHUNKS, RANK, WIDE), summed, *others, inverse))
        right_other = shift(right, core=1)
    with jax.named_scope("error"):
        (part,) = error_part(merged, left_wide, right)
        error_new, right_turned = error_part(merged, left_wide, right_other, right, part)
    return (error_new, left_turned.T, right_turned.T)


def solution(mesh):
    fine = Mesh(mesh.devices.reshape(SIZES), AXES)
    rows = ("x", "zhi", "core")
    return jax.shard_map(
        body,
        mesh=fine,
        in_specs=(P(("zlo", "y"), rows, None), P(("zlo", "y"), rows, None), P(rows, None)),
        out_specs=(P(("zlo", "y"), rows, None), P(rows, None), P(rows, None)),
        check_vma=False,
    )
```
